768 devices in a mesh: dp: 16 (over x, y_lo), blocks: 48 (over z, y_hi, core).
Axes of the slice: x: 4, y: 8 (y_hi: 2, y_lo: 4; y = y_hi * 4 + y_lo), z: 12, core: 2. Of those that a mesh axis runs over, the one named last changes fastest.
Arguments:
- grads: bfloat16 [16, 336, 512, 512], P('dp', 'blocks'), may hold values from -640 to 640, as said below
- owner: int32 [336, 1], P('blocks'), may hold values from 0 to 15; in each aligned block of 7 rows (0 to 6, 7 to 13, ...) at most 2 rows name the same one
Outputs:
- owned_roots: bfloat16 [48, 16, 2, 512, 512], P('blocks', 'dp')
The draws below stay inside these ranges and needn't reach their ends.
Inputs may be any that keep to these rules, and one draw needn't show every extreme that they name: `grads`: gradient entries are finite. `owner`: among the 7 blocks of one column (aligned blocks of 7 rows), no dp index is named more than 2 times, and some column names one exactly 2 times.
All inputs are finite; a program needn't handle non-finite values.
Results may differ from the reference program's by a relative error of at most 0.015.
Values may be sent and summed in bfloat16 or wider, within the bound.
A program may use at most 32 MiB of HBM per device.

```python
import math
import jax
import jax.numpy as jnp
import numpy as np
from jax import lax

BS = 512
BPC = 7
CAP = 2
ITERS = 2
REPLICAS = 16
NB = 336
N_BLOCKS = 48


def draw_grads(key, part):
    key = jax.random.fold_in(key, 7)
    k_base = jax.random.fold_in(key, 0)
    k_row = jax.random.fold_in(key, 1)
    k_col = jax.random.fold_in(key, 2)
    k_blk = jax.random.fold_in(key, 3)
    k_pick = jax.random.fold_in(key, 5)
    k_lead = jax.random.fold_in(key, 6)
    full_shape = (REPLICAS, NB, BS, BS)
    base_draw = jnp.clip(jax.random.normal(k_base, full_shape, jnp.float32), -4.0, 4.0)
    half_decade = 0.5 * math.log(10.0)
    row_scale = jnp.exp(half_decade * jax.random.uniform(k_row, (REPLICAS, NB, BS, 1), jnp.float32))
    col_scale = jnp.exp(half_decade * jax.random.uniform(k_col, (REPLICAS, NB, 1, BS), jnp.float32))
    blk_scale = jnp.exp(math.log(2.0) * jax.random.uniform(k_blk, (REPLICAS, NB, 1, 1), jnp.float32))
    rise_scale = jnp.exp(0.5 * math.log(3.0) * jnp.arange(NB, dtype=jnp.float32) / NB)[None, :, None, None]
    quiet_count = max(1, REPLICAS // 4)
    ranking = jax.random.permutation(k_pick, REPLICAS)
    replica_scale = jnp.where(ranking < quiet_count, 0.02, 1.0).astype(jnp.float32)[:, None]
    leader = jax.random.randint(k_lead, (NB,), 0, REPLICAS)
    is_lead = jnp.arange(REPLICAS, dtype=jnp.int32)[:, None] == leader[None, :]
    pair_scale = jnp.where(is_lead, 4.0, replica_scale).astype(jnp.float32)[:, :, None, None]
    return (base_draw * row_scale * col_scale * blk_scale * rise_scale * pair_scale).astype(jnp.bfloat16)


def shared_out(key, own, number, rows, amount, top, bound, skew):
    order = jax.random.permutation(key, amount)
    crowded, ordinary = load_shares(amount, rows * top, bound, skew, True), load_shares(amount, rows * top, bound, skew, False)
    places = jnp.arange(amount)

    def named(sizes, rotation):
        used = int((sizes > 0).sum())
        fixed = max(1, used // 4)
        moved = fixed + (places - fixed + rotation * (used - fixed)) % max(1, amount - fixed)
        return jnp.zeros((amount,), jnp.int32).at[order[jnp.where(places < fixed, places, moved)]].set(jnp.asarray(sizes, jnp.int32))

    sizes = jnp.where(number % 4 == 0, named(crowded, number // 4), named(ordinary, number - number // 4 - 1))
    mixed = jax.random.permutation(jax.random.fold_in(own, 3), amount)
    source_of, taker = mixed[0:amount // 2 * 2:2], mixed[1:amount // 2 * 2:2]
    margin = jnp.minimum(sizes[source_of] - 1, bound - sizes[taker]) // 2
    margin = jnp.where((source_of == order[0]) | (taker == order[0]) | (sizes[taker] == 0), 0, jnp.maximum(margin, 0))
    moved = jax.random.randint(jax.random.fold_in(own, 4), (amount // 2,), 0, 1 << 20) % (margin + 1)
    sizes = sizes.at[source_of].add(-moved).at[taker].add(moved)
    members = jnp.searchsorted(jnp.cumsum(sizes), jnp.arange(rows * top), side="right").astype(jnp.int32)
    listing = members.reshape(top, rows).T
    listing = listing[jax.random.permutation(jax.random.fold_in(own, 1), rows)]
    rotation = jax.random.randint(jax.random.fold_in(own, 2), (rows, 1), 0, top)
    return jnp.take_along_axis(listing, (jnp.arange(top)[None, :] + rotation) % top, axis=1)


def load_shares(number_of, total, reach, skew, full):
    portions = [(1 << 20) // math.isqrt(grade ** skew) + 1 for grade in range(1, number_of + 1)]
    largest = reach if full else min(reach, max(-(-total // number_of), total * portions[0] // sum(portions)))
    least = 1 if total - largest >= number_of - 1 else 0
    given, rest = [largest] + [least] * (number_of - 1), total - largest - least * (number_of - 1)
    while rest > 0:
        movable = [i for i in range(1, number_of) if given[i] < largest] or [i for i in range(1, number_of) if given[i] < reach]
        whole, left = sum([portions[i] for i in movable]), rest
        for i in movable:
            extra = min(reach - given[i], max(1, left * portions[i] // whole), rest)
            given[i] = given[i] + extra
            rest = rest - extra
    return np.array(given)


def setup_inputs(seed: int = 0) -> dict:
    key_list = jax.random.split(jax.random.key(seed), 3)
    grads = draw_grads(jax.random.fold_in(key_list[2], 71), 0)
    owner_keys = jax.random.split(jax.random.fold_in(key_list[1], 1), NB // BPC)
    owner_turns = jax.random.permutation(jax.random.fold_in(key_list[1], 3), NB // BPC)
    owner = jax.vmap(lambda own, number: shared_out(jax.random.fold_in(key_list[1], 2), own, number, BPC, REPLICAS, 1, CAP, 2))(owner_keys, owner_turns).reshape((NB, 1))
    return {"grads": grads, "owner": owner}


clip_level = 0.25
ridge = 0.02

def product(left, right):
    return jnp.einsum('nik,nkj->nij', left.astype(jnp.float32), right.astype(jnp.float32), precision=lax.Precision.HIGHEST)

def newton(stat_bf):
    order = stat_bf.shape[-1]
    unit = jnp.eye(order, dtype=jnp.float32)
    stat_f = stat_bf.astype(jnp.float32)
    scale_z = 0.5 * order ** 0.5 * lax.rsqrt(lax.optimization_barrier(jnp.sum(stat_f * stat_f, axis=(1, 2))) + 1e-06)[:, None, None]
    coupled = scale_z * stat_f
    iterate = None
    for step in range(ITERS):
        factor = ((5.0 * unit - coupled) * 0.25).astype(jnp.bfloat16)
        if step == 0:
            iterate = (jnp.sqrt(jnp.sqrt(scale_z)) * factor.astype(jnp.float32)).astype(jnp.bfloat16)
        else:
            iterate = product(iterate, factor).astype(jnp.bfloat16)
        if step + 1 < ITERS:
            square_t = product(factor, factor).astype(jnp.bfloat16)
            fourth_t = product(square_t, square_t).astype(jnp.bfloat16)
            coupled = product(fourth_t, coupled.astype(jnp.bfloat16))
    return iterate

def slot_table(owner_col, replicas):
    count = owner_col.shape[0]
    position = jnp.arange(count, dtype=jnp.int32)
    same = owner_col[:, None] == owner_col[None, :]
    earlier = position[None, :] < position[:, None]
    slot_rank = lax.optimization_barrier(jnp.sum((same & earlier).astype(jnp.int32), axis=1))
    targets = jnp.arange(replicas, dtype=jnp.int32)
    slots = jnp.arange(CAP, dtype=jnp.int32)
    hit = (owner_col[None, None, :] == targets[:, None, None]) & (slot_rank[None, None, :] == slots[None, :, None])
    return hit.astype(jnp.float32)

def reference(grads, owner):
    entries = NB * BS * BS
    columns = jnp.arange(N_BLOCKS, dtype=jnp.int32)

    def column_sq(column):
        piece = lax.dynamic_slice_in_dim(grads, column * BPC, BPC, 1).astype(jnp.float32)
        return lax.optimization_barrier(jnp.sum(piece * piece, axis=(1, 2, 3)))
    total_sq = lax.optimization_barrier(jnp.sum(lax.map(column_sq, columns), axis=0))
    scale = jnp.minimum(1.0, clip_level * lax.rsqrt(total_sq / entries + 1e-06))
    weight = scale * scale / (REPLICAS * BS)
    unit = jnp.eye(BS, dtype=jnp.float32)

    def column_roots(column):
        piece = lax.dynamic_slice_in_dim(grads, column * BPC, BPC, 1)
        owner_col = lax.dynamic_slice_in_dim(owner, column * BPC, BPC, 0)[:, 0]

        def add_replica(replica, total):
            grad_blk = lax.dynamic_index_in_dim(piece, replica, 0, keepdims=False).astype(jnp.float32)
            outer = jnp.einsum('jrc,jkc->jrk', grad_blk, grad_blk, precision=lax.Precision.HIGHEST)
            rounded = lax.optimization_barrier((weight[replica] * outer).astype(jnp.bfloat16))
            return total + rounded.astype(jnp.float32)
        summed = lax.fori_loop(0, REPLICAS, add_replica, jnp.zeros((BPC, BS, BS), jnp.float32))
        stat_bf = (summed + ridge * unit).astype(jnp.bfloat16)
        roots = newton(stat_bf)
        onehot = slot_table(owner_col, REPLICAS)
        return jnp.einsum('osj,jrc->osrc', onehot, roots.astype(jnp.float32), precision=lax.Precision.HIGHEST).astype(jnp.bfloat16)
    return lax.map(column_roots, columns)
```

```python
import functools

import jax
import jax.numpy as jnp
from jax import lax
from jax.experimental import pallas as pl
from jax.experimental.pallas import tpu as pltpu
from jax.sharding import PartitionSpec as P

CAP = 2
CLIP = 0.25
RIDGE = 0.02
T = 128
QUARTER = 256
PIECE = 64
NX = 4
NY = 4
NC = 4
MESH = pl.DeviceIdType.MESH
F32 = jnp.float32
BF16 = jnp.bfloat16


def gram(left, right):
    return lax.dot_general(left, right, (((1,), (1,)), ((), ())), preferred_element_type=F32)


def exchange_kernel(
    n_blocks, count, entries,
    owner_ref, grads_ref,
    pieces_out, diag_out,
    g_buf, packed, xr1, xr2, xr3, xs2, xsum, yr, stat, a2a_send, zbuf, cbuf, wbuf, ebuf, eybuf, slot_idx,
    g_sem, x_send, x_recv, y_send, y_recv, a_send, a_recv, z_send, z_recv, c_send, c_recv, w_send, w_recv,
    e_send, e_recv, ey_send, ey_recv, out_sem,
):
    nz = n_blocks // NC
    me = lax.axis_index("dp")
    col = lax.axis_index("blocks")
    x, y = me // NY, me % NY
    z, c = col // NC, col % NC

    def dp_id(xx, yy):
        return {"dp": xx * NY + yy, "blocks": col}

    def col_id(zz, cc):
        return {"dp": me, "blocks": zz * NC + cc}

    right, left = lax.rem(x + 1, NX), lax.rem(x + NX - 1, NX)
    opposite = lax.rem(x + 2, NX)

    def remote(src, dst, ssem, rsem, dev):
        return pltpu.make_async_remote_copy(
            src_ref=src, dst_ref=dst, send_sem=ssem, recv_sem=rsem, device_id=dev, device_id_type=MESH
        )

    def load(j):
        return pltpu.make_async_copy(grads_ref.at[0, j], g_buf.at[j], g_sem.at[j])

    for j in range(count):
        load(j).start()

    barrier = pltpu.get_barrier_semaphore()

    @pl.loop(1, NX * NY)
    def _(k):
        peer = lax.rem(me + k, NX * NY)
        pl.semaphore_signal(barrier, inc=1, device_id={"dp": peer, "blocks": col}, device_id_type=MESH)

    if nz > 1:
        @pl.loop(1, nz)
        def _(k):
            pl.semaphore_signal(barrier, inc=1, device_id=col_id(lax.rem(z + k, nz), c), device_id_type=MESH)

    @pl.loop(1, NC)
    def _(k):
        pl.semaphore_signal(barrier, inc=1, device_id=col_id(z, lax.rem(c + k, NC)), device_id_type=MESH)

    pl.semaphore_wait(barrier, NX * NY - 1 + nz - 1 + NC - 1)

    def x_copy(kind, j):
        half_a, half_b = pl.ds(0, T), pl.ds(T, T)
        src = {
            0: lambda: packed.at[j, opposite, half_a],
            1: lambda: packed.at[j, opposite, half_b],
            2: lambda: packed.at[j, right, half_b],
            3: lambda: packed.at[j, left, half_a],
            4: lambda: xs2.at[0, j],
            5: lambda: xs2.at[1, j],
        }[kind]()
        dst = {0: xr1, 1: xr1, 2: xr3, 3: xr3, 4: xr2, 5: xr2}[kind].at[kind % 2, j]
        to = right if kind % 2 == 0 else left
        return remote(src, dst, x_send.at[kind, j], x_recv.at[kind, j], dp_id(to, y))

    rows = lax.broadcasted_iota(jnp.int32, (T, T), 0)
    cols = lax.broadcasted_iota(jnp.int32, (T, T), 1)
    lower = rows >= cols
    eye = rows == cols

    zbuf[z] = jnp.zeros((8, T), F32)
    ebuf[x] = jnp.zeros((16, T), F32)

    @pl.loop(0, count)
    def _(j):
        load(j).wait()
        top, bottom = g_buf[j, :256], g_buf[j, 256:]
        cross = gram(bottom, top)
        for t, (r, k) in enumerate(((0, 0), (0, 1), (1, 0), (1, 1))):
            packed[j, t // 2, (t % 2) * T:(t % 2 + 1) * T, :] = cross[
                r * T:(r + 1) * T, k * T:(k + 1) * T
            ].astype(BF16)
        square = jnp.zeros((T, T), F32)
        for h, part in enumerate((top, bottom)):
            own = gram(part, part)
            d0, d1 = own[:T, :T], own[T:, T:]
            packed[j, 2, h * T:(h + 1) * T, :] = own[T:, :T].astype(BF16)
            packed[j, 3, h * T:(h + 1) * T, :] = jnp.where(lower, d0, d1).astype(BF16)
            e1 = jnp.where(eye, d1, 0.0)
            ebuf[x, pl.ds(2 * j + h, 1), :] = jnp.sum(e1, axis=0, keepdims=True)
            square = square + jnp.where(eye, d0, 0.0) + e1
        zbuf[z] += jnp.sum(square.reshape(T // 8, 8, T), axis=0)
        x_copy(0, j).start()
        x_copy(1, j).start()

    def z_copy(k, incoming):
        peer = lax.rem(z + k, nz)
        at = peer if incoming else z
        return remote(zbuf.at[at], zbuf.at[at], z_send.at[k], z_recv.at[at], col_id(peer, c))

    def c_copy(k, incoming):
        peer = lax.rem(c + k, NC)
        at = peer if incoming else c
        return remote(cbuf.at[at], cbuf.at[at], c_send.at[k], c_recv.at[at], col_id(z, peer))

    def w_copy(k, incoming):
        peer = lax.rem(x + k, NX)
        at = peer if incoming else x
        return remote(wbuf.at[at], wbuf.at[at], w_send.at[k], w_recv.at[at], dp_id(peer, y))

    def e_copy(k, incoming):
        peer = lax.rem(x + k, NX)
        at = peer if incoming else x
        return remote(ebuf.at[at], ebuf.at[at], e_send.at[k], e_recv.at[at], dp_id(peer, y))

    def ey_copy(k, incoming):
        peer = lax.rem(y + k, NY)
        at = peer if incoming else y
        return remote(eybuf.at[at], eybuf.at[at], ey_send.at[k], ey_recv.at[at], dp_id(x, peer))

    if nz > 1:
        @pl.loop(1, nz)
        def _(k):
            z_copy(k, False).start()

    @pl.loop(1, NX)
    def _(k):
        e_copy(k, False).start()

    @pl.loop(0, count)
    def _(j):
        x_copy(2, j).start()
        x_copy(3, j).start()

    @pl.loop(0, NX * NY * CAP)
    def _(i):
        target, slot = i // CAP, i % CAP
        found = jnp.int32(count)
        seen = jnp.int32(0)
        for j in range(count):
            hit = owner_ref[j, 0] == target
            found = jnp.where(jnp.logical_and(hit, seen == slot), j, found)
            seen = seen + jnp.where(hit, 1, 0)
        slot_idx[i] = found

    stat[count] = jnp.zeros((PIECE, T), BF16)

    if nz > 1:
        @pl.loop(1, nz)
        def _(k):
            z_copy(k, True).wait_recv()

    cbuf[c] = jnp.sum(zbuf[...], axis=0)

    @pl.loop(1, NC)
    def _(k):
        c_copy(k, False).start()

    @pl.loop(1, NC)
    def _(k):
        c_copy(k, True).wait_recv()

    total = jnp.sum(jnp.sum(cbuf[...], axis=0), axis=(0, 1), keepdims=True)
    scale = jnp.minimum(1.0, CLIP * lax.rsqrt(jnp.broadcast_to(total, (8, T)) / entries + 1e-06))
    wbuf[x] = scale * scale / (NX * NY * 512)

    @pl.loop(1, NX)
    def _(k):
        w_copy(k, False).start()

    @pl.loop(1, NX)
    def _(k):
        w_copy(k, True).wait_recv()

    w_me, w_left, w_right = wbuf[x, 0:1, :], wbuf[left, 0:1, :], wbuf[right, 0:1, :]

    def wide(value):
        return value.astype(F32)

    @pl.loop(0, count)
    def _(j):
        x_copy(0, j).wait_recv()
        xs2[0, j] = (w_left * wide(xr1[0, j]) + w_me * wide(packed[j, right, :T, :])).astype(BF16)
        x_copy(4, j).start()
        x_copy(1, j).wait_recv()
        xs2[1, j] = (w_right * wide(xr1[1, j]) + w_me * wide(packed[j, left, T:, :])).astype(BF16)
        x_copy(5, j).start()

    @pl.loop(1, NX)
    def _(k):
        e_copy(k, True).wait_recv()

    diag = jnp.zeros((16, T), F32)
    for k in range(NX):
        diag = diag + wbuf[k, 0:1, :] * ebuf[k]
    eybuf[y] = diag

    @pl.loop(1, NY)
    def _(k):
        ey_copy(k, False).start()

    def y_copy(k, j, incoming):
        peer = lax.rem(y + k, NY)
        at = peer if incoming else y
        piece = pl.ds(pl.multiple_of(peer * PIECE, PIECE), PIECE)
        return remote(xsum.at[j, piece], yr.at[j, at], y_send.at[k, j], y_recv.at[j, at], dp_id(x, peer))

    @pl.loop(0, count)
    def _(j):
        for kind in (2, 3, 4, 5):
            x_copy(kind, j).wait_recv()
        half_a = w_me * wide(packed[j, x, :T, :]) + wide(xr2[0, j]) + w_right * wide(xr3[1, j])
        half_b = w_me * wide(packed[j, x, T:, :]) + wide(xr2[1, j]) + w_left * wide(xr3[0, j])
        xsum[j, :T, :] = half_a.astype(BF16)
        xsum[j, T:, :] = half_b.astype(BF16)
        yr[j, y] = xsum[j, pl.ds(pl.multiple_of(y * PIECE, PIECE), PIECE), :]
        for k in range(1, NY):
            y_copy(k, j, False).start()

    packed_row = me * PIECE + lax.broadcasted_iota(jnp.int32, (PIECE, T), 0)
    on_diagonal = jnp.logical_and(packed_row >= 6 * T, packed_row % T == lax.broadcasted_iota(jnp.int32, (PIECE, T), 1))
    ridge = jnp.where(on_diagonal, RIDGE, 0.0).astype(F32)

    @pl.loop(0, count)
    def _(j):
        for k in range(1, NY):
            y_copy(k, j, True).wait_recv()
        got = wide(yr[j, 0]) + wide(yr[j, 1]) + wide(yr[j, 2]) + wide(yr[j, 3])
        stat[j] = (got + ridge).astype(BF16)

    @pl.loop(0, NX * NY)
    def _(o):
        for s in range(CAP):
            a2a_send[o, s] = stat[slot_idx[o * CAP + s]]

    def a_copy(k, incoming):
        peer = lax.rem(me + k, NX * NY)
        at = peer if incoming else me
        return remote(a2a_send.at[peer], pieces_out.at[at], a_send.at[k], a_recv.at[at], {"dp": peer, "blocks": col})

    @pl.loop(1, NX * NY)
    def _(k):
        a_copy(k, False).start()

    mine = pltpu.make_async_copy(a2a_send.at[me], pieces_out.at[me], out_sem)
    mine.start()

    @pl.loop(1, NY)
    def _(k):
        ey_copy(k, True).wait_recv()

    diag_out[...] = eybuf[0] + eybuf[1] + eybuf[2] + eybuf[3]

    if nz > 1:
        @pl.loop(1, nz)
        def _(k):
            z_copy(k, False).wait_send()

    @pl.loop(1, NX)
    def _(k):
        c_copy(k, False).wait_send()
        w_copy(k, False).wait_send()
        e_copy(k, False).wait_send()
        ey_copy(k, False).wait_send()

    @pl.loop(0, count)
    def _(j):
        for kind in range(6):
            x_copy(kind, j).wait_send()
        for k in range(1, NY):
            y_copy(k, j, False).wait_send()

    @pl.loop(1, NX * NY)
    def _(k):
        a_copy(k, True).wait_recv()
        a_copy(k, False).wait_send()

    mine.wait()


def product(left, right):
    return lax.dot_general(left, right, (((1,), (0,)), ((), ())), preferred_element_type=F32)


def newton_kernel(count, owner_ref, index_ref, pieces_ref, diag_ref, out_ref, mat):
    order = mat.shape[-1]
    me = index_ref[0]
    rows = lax.broadcasted_iota(jnp.int32, (T, T), 0)
    cols = lax.broadcasted_iota(jnp.int32, (T, T), 1)
    unit5 = jnp.where(
        lax.broadcasted_iota(jnp.int32, (order, order), 0) == lax.broadcasted_iota(jnp.int32, (order, order), 1), 5.0, 0.0
    ).astype(F32)
    for s in range(CAP):
        found = jnp.int32(0)
        seen = jnp.int32(0)
        for j in range(count):
            hit = owner_ref[j, 0] == me
            found = jnp.where(jnp.logical_and(hit, seen == s), j, found)
            seen = seen + jnp.where(hit, 1, 0)
        live = seen > s

        def tile(t):
            return jnp.concatenate([pieces_ref[2 * t, s], pieces_ref[2 * t + 1, s]], axis=0).astype(F32)

        def put(r, k, value):
            mat[s, r * T:(r + 1) * T, k * T:(k + 1) * T] = value

        for t, (r, k) in enumerate(((2, 0), (2, 1), (3, 0), (3, 1), (1, 0), (3, 2))):
            value = tile(t)
            put(r, k, value)
            put(k, r, value.T)
        for h in range(2):
            value = tile(6 + h)
            turned = value.T
            edge = (diag_ref[pl.ds(2 * found + h, 1), :] + RIDGE).astype(BF16).astype(F32)
            put(2 * h, 2 * h, jnp.where(rows >= cols, value, turned))
            put(2 * h + 1, 2 * h + 1, jnp.where(rows < cols, value, jnp.where(rows == cols, edge, turned)))
        full = mat[s]
        z = 0.5 * order**0.5 * lax.rsqrt(jnp.sum(full * full, axis=(0, 1), keepdims=True) + 1e-06)
        coupled = z * full
        factor = ((unit5 - coupled) * 0.25).astype(BF16)
        iterate = (jnp.sqrt(jnp.sqrt(z)) * factor.astype(F32)).astype(BF16)
        square = product(factor, factor).astype(BF16)
        fourth = product(square, square).astype(BF16)
        coupled = product(fourth, coupled.astype(BF16))
        factor = ((unit5 - coupled) * 0.25).astype(BF16)
        root = product(iterate, factor)
        out_ref[s] = jnp.where(live, root, 0.0).astype(BF16)


def body(n_blocks, grads, owner):
    count, order = grads.shape[1], grads.shape[2]
    entries = n_blocks * count * order * order
    n = NX * NY
    nz = n_blocks // NC
    dma = pltpu.SemaphoreType.DMA
    vmem = pltpu.VMEM
    pieces, diag = pl.pallas_call(
        functools.partial(exchange_kernel, n_blocks, count, float(entries)),
        out_shape=(
            jax.ShapeDtypeStruct((n, CAP, PIECE, T), BF16),
            jax.ShapeDtypeStruct((16, T), F32),
        ),
        in_specs=[pl.BlockSpec(memory_space=pltpu.SMEM), pl.BlockSpec(memory_space=pl.ANY)],
        out_specs=(pl.BlockSpec(memory_space=pl.ANY), pl.BlockSpec(memory_space=pltpu.VMEM)),
        scratch_shapes=[
            vmem((count, order, order), BF16),
            vmem((count, NX, QUARTER, T), BF16),
            vmem((2, count, T, T), BF16),
            vmem((2, count, T, T), BF16),
            vmem((2, count, T, T), BF16),
            vmem((2, count, T, T), BF16),
            vmem((count, QUARTER, T), BF16),
            vmem((count, NY, PIECE, T), BF16),
            vmem((count + 1, PIECE, T), BF16),
            vmem((n, CAP, PIECE, T), BF16),
            vmem((nz, 8, T), F32),
            vmem((NC, 8, T), F32),
            vmem((NX, 8, T), F32),
            vmem((NX, 16, T), F32),
            vmem((NY, 16, T), F32),
            pltpu.SMEM((n * CAP,), jnp.int32),
            dma((count,)),
            dma((6, count)), dma((6, count)),
            dma((NY, count)), dma((count, NY)),
            dma((n,)), dma((n,)),
            dma((nz,)), dma((nz,)),
            dma((NC,)), dma((NC,)),
            dma((NX,)), dma((NX,)),
            dma((NX,)), dma((NX,)),
            dma((NY,)), dma((NY,)),
            dma(()),
        ],
        compiler_params=pltpu.CompilerParams(
            collective_id=0, has_side_effects=True, vmem_limit_bytes=32 * 1024 * 1024
        ),
        cost_estimate=pl.CostEstimate(flops=2 * count * order**3, bytes_accessed=grads.size * 2, transcendentals=0),
        name="exchange",
    )(owner, grads)
    index = lax.axis_index("dp").reshape(1).astype(jnp.int32)
    roots = pl.pallas_call(
        functools.partial(newton_kernel, count),
        out_shape=jax.ShapeDtypeStruct((CAP, order, order), BF16),
        in_specs=[
            pl.BlockSpec(memory_space=pltpu.SMEM),
            pl.BlockSpec(memory_space=pltpu.SMEM),
            pl.BlockSpec(memory_space=pltpu.VMEM),
            pl.BlockSpec(memory_space=pltpu.VMEM),
        ],
        out_specs=pl.BlockSpec(memory_space=pltpu.VMEM),
        scratch_shapes=[vmem((CAP, order, order), F32)],
        compiler_params=pltpu.CompilerParams(vmem_limit_bytes=32 * 1024 * 1024),
        cost_estimate=pl.CostEstimate(flops=16 * order**3, bytes_accessed=4 * order * order, transcendentals=0),
        name="newton",
    )(owner, index, pieces, diag)
    return roots[None, None]


def solution(mesh):
    return jax.shard_map(
        functools.partial(body, mesh.shape["blocks"]),
        mesh=mesh,
        in_specs=(P("dp", "blocks", None, None), P("blocks", None)),
        out_specs=P("blocks", "dp", None, None, None),
        check_vma=False,
    )
```

```python
import functools

import jax
import jax.numpy as jnp
from jax import lax
from jax.experimental import pallas as pl
from jax.experimental.pallas import tpu as pltpu
from jax.sharding import PartitionSpec as P

CAP = 2
CLIP = 0.25
RIDGE = 0.02
T = 128
QUARTER = 256
PIECE = 64
NX = 4
NY = 4
NC = 4
X_FIRST = 5
MESH = pl.DeviceIdType.MESH
F32 = jnp.float32
BF16 = jnp.bfloat16


def gram(left, right):
    return lax.dot_general(left, right, (((1,), (1,)), ((), ())), preferred_element_type=F32)


def exchange_kernel(
    n_blocks, count, entries,
    owner_ref, grads_ref,
    pieces_out, diag_out,
    g_buf, packed, first_x, first_y, sum_x, sum_y, second_x, second_y, stat, a2a_send,
    zbuf, cbuf, wbuf, ebuf, eybuf, slot_idx,
    g_sem, sems,
):
    nz = n_blocks // NC
    order = g_buf.shape[-1]
    n_x, n_y = min(X_FIRST, count), count - min(X_FIRST, count)
    me = lax.axis_index("dp")
    col = lax.axis_index("blocks")
    x, y = me // NY, me % NY
    z, c = col // NC, col % NC

    def device(xx, yy, zz, cc):
        return {"dp": xx * NY + yy, "blocks": zz * NC + cc}

    def x_peer(k):
        return lax.rem(x + k, NX)

    def y_peer(k):
        return lax.rem(y + k, NY)

    def c_peer(k):
        return lax.rem(c + k, NC)

    Z, C, X1, Y1, X2, Y2, E1, E2, A2A, OWN = range(10)

    def send(group, src, dst, dev):
        pltpu.make_async_remote_copy(
            src_ref=src, dst_ref=dst, send_sem=sems.at[0, group], recv_sem=sems.at[1, group],
            device_id=dev, device_id_type=MESH,
        ).start()

    def whole(group, like):
        return pltpu.make_async_remote_copy(
            src_ref=like, dst_ref=like, send_sem=sems.at[0, group], recv_sem=sems.at[1, group],
            device_id=device(x_peer(1), y, z, c), device_id_type=MESH,
        )

    def load(j):
        return pltpu.make_async_copy(grads_ref.at[0, j], g_buf.at[j], g_sem.at[j])

    barrier = pltpu.get_barrier_semaphore()

    def greet(dev):
        pl.semaphore_signal(barrier, inc=1, device_id=dev, device_id_type=MESH)

    def z_peers(act):
        if nz > 1:
            @pl.loop(1, nz)
            def _(k):
                act(lax.rem(z + k, nz))

    def plane_peers(act):
        @pl.loop(1, NX * NY)
        def _(k):
            act(lax.rem(me + k, NX * NY))

    def weight_peers(act, own_c):
        @pl.loop(0 if own_c else 1, NC)
        def _(k):
            @pl.loop(1, NX)
            def _(i):
                act(device(x_peer(i), y, z, c_peer(k)), 0)
                act(device(x, y_peer(i), z, c_peer(k)), 1)

        @pl.loop(1, NC)
        def _(k):
            act(device(x, y, z, c_peer(k)), 0)

    z_peers(lambda p: greet(device(x, y, p, c)))
    weight_peers(lambda dev, axis: greet(dev), False)
    plane_peers(lambda p: greet({"dp": p, "blocks": col}))
    for j in range(count):
        load(j).start()

    rows = lax.broadcasted_iota(jnp.int32, (T, T), 0)
    cols = lax.broadcasted_iota(jnp.int32, (T, T), 1)
    lower = rows >= cols
    eye = rows == cols
    zbuf[z] = jnp.zeros((8, T), F32)
    ebuf[x] = jnp.zeros((16, T), F32)

    @pl.loop(0, count)
    def _(j):
        load(j).wait()
        top, bottom = g_buf[j, :256], g_buf[j, 256:]
        square = jnp.zeros((T, T), F32)
        for h, part in enumerate((top, bottom)):
            own = gram(part, part)
            d0, d1 = own[:T, :T], own[T:, T:]
            packed[j, 2, h * T:(h + 1) * T, :] = own[T:, :T].astype(BF16)
            packed[j, 3, h * T:(h + 1) * T, :] = jnp.where(lower, d0, d1).astype(BF16)
            e1 = jnp.where(eye, d1, 0.0)
            ebuf[x, pl.ds(2 * j + h, 1), :] = jnp.sum(e1, axis=0, keepdims=True)
            square = square + jnp.where(eye, d0, 0.0) + e1
        zbuf[z] += jnp.sum(square.reshape(T // 8, 8, T), axis=0)
        cross = gram(bottom, top)
        for t, (r, k) in enumerate(((0, 0), (0, 1), (1, 0), (1, 1))):
            packed[j, t // 2, (t % 2) * T:(t % 2 + 1) * T, :] = cross[
                r * T:(r + 1) * T, k * T:(k + 1) * T
            ].astype(BF16)

    pl.semaphore_wait(barrier, NX * NY - 1 + nz - 1 + (NX + NY - 1) * (NC - 1))

    z_peers(lambda p: send(Z, zbuf.at[z], zbuf.at[z], device(x, y, p, c)))

    @pl.loop(0, n_x)
    def _(j):
        @pl.loop(1, NX)
        def _(k):
            to = x_peer(k)
            send(X1, packed.at[j, to], first_x.at[x, j], device(to, y, z, c))

    if n_y:
        @pl.loop(0, n_y)
        def _(j):
            @pl.loop(1, NY)
            def _(k):
                to = y_peer(k)
                send(Y1, packed.at[n_x + j, to], first_y.at[y, j], device(x, to, z, c))

    @pl.loop(1, NX)
    def _(k):
        send(E1, ebuf.at[x], ebuf.at[x], device(x_peer(k), y, z, c))

    @pl.loop(0, NX * NY * CAP)
    def _(i):
        target, slot = i // CAP, i % CAP
        found = jnp.int32(count)
        seen = jnp.int32(0)
        for j in range(count):
            hit = owner_ref[j] == target
            found = jnp.where(jnp.logical_and(hit, seen == slot), j, found)
            seen = seen + jnp.where(hit, 1, 0)
        slot_idx[i] = found

    stat[count] = jnp.zeros((PIECE, T), BF16)

    if nz > 1:
        whole(Z, zbuf.at[pl.ds(0, nz - 1)]).wait_recv()
    total = jnp.sum(zbuf[...], axis=0)
    cbuf[x * NC + c] = total
    cbuf[(NX + y) * NC + c] = total

    def send_sum(dev, axis):
        mine = x if axis == 0 else NX + y
        send(C, cbuf.at[x * NC + c], cbuf.at[mine * NC + c], dev)

    weight_peers(send_sum, True)
    c_like = cbuf.at[pl.ds(0, NX * NC - 1 + (NY - 1) * NC)]
    whole(C, c_like).wait_recv()

    along_x = [jnp.sum(jnp.sum(cbuf[k * NC:(k + 1) * NC], axis=0), axis=0, keepdims=True) for k in range(NX)]
    along_y = [jnp.sum(jnp.sum(cbuf[(NX + k) * NC:(NX + k + 1) * NC], axis=0), axis=0, keepdims=True) for k in range(NY)]
    sums = jnp.sum(jnp.concatenate(along_x + along_y, axis=0), axis=1, keepdims=True)
    scale = jnp.minimum(1.0, CLIP * lax.rsqrt(jnp.broadcast_to(sums, (NX + NY, T)) / entries + 1e-06))
    wbuf[...] = scale * scale / (NX * NY * order)

    def weight_x(k):
        return wbuf[pl.ds(k, 1), :]

    def weight_y(k):
        return wbuf[pl.ds(NX + k, 1), :]

    def wide(value):
        return value.astype(F32)

    whole(X1, first_x.at[pl.ds(0, NX - 1)]).wait_recv()

    @pl.loop(0, n_x)
    def _(j):
        got = weight_x(x) * wide(packed[j, x])
        for k in range(1, NX):
            got = got + weight_x(x_peer(k)) * wide(first_x[x_peer(k), j])
        sum_x[j] = got.astype(BF16)
        for k in range(1, NY):
            to = y_peer(k)
            piece = pl.ds(pl.multiple_of(to * PIECE, PIECE), PIECE)
            send(X2, sum_x.at[j, piece], second_x.at[y, j], device(x, to, z, c))

    if n_y:
        whole(Y1, first_y.at[pl.ds(0, NY - 1)]).wait_recv()

        @pl.loop(0, n_y)
        def _(j):
            got = weight_x(x) * wide(packed[n_x + j, y])
            for k in range(1, NY):
                got = got + weight_y(y_peer(k)) * wide(first_y[y_peer(k), j])
            sum_y[j] = got.astype(BF16)
            for k in range(1, NX):
                to = x_peer(k)
                piece = pl.ds(pl.multiple_of(to * PIECE, PIECE), PIECE)
                send(Y2, sum_y.at[j, piece], second_y.at[x, j], device(to, y, z, c))

    whole(E1, ebuf.at[pl.ds(0, NX - 1)]).wait_recv()
    diag = jnp.zeros((16, T), F32)
    for k in range(NX):
        diag = diag + wbuf[k:k + 1, :] * ebuf[k]
    eybuf[y] = diag

    @pl.loop(1, NY)
    def _(k):
        send(E2, eybuf.at[y], eybuf.at[y], device(x, y_peer(k), z, c))

    lane = lax.broadcasted_iota(jnp.int32, (PIECE, T), 1)
    row = lax.broadcasted_iota(jnp.int32, (PIECE, T), 0)

    def ridge(position):
        packed_row = position * PIECE + row
        on_diagonal = jnp.logical_and(packed_row >= 6 * T, packed_row % T == lane)
        return jnp.where(on_diagonal, RIDGE, 0.0).astype(F32)

    if n_y:
        whole(Y2, second_y.at[pl.ds(0, NX - 1)]).wait_recv()
        ridge_y = ridge(y * NX + x)

        @pl.loop(0, n_y)
        def _(j):
            got = wide(sum_y[j, pl.ds(pl.multiple_of(x * PIECE, PIECE), PIECE), :])
            for k in range(1, NX):
                got = got + wide(second_y[x_peer(k), j])
            stat[n_x + j] = (got + ridge_y).astype(BF16)

    whole(X2, second_x.at[pl.ds(0, NY - 1)]).wait_recv()
    ridge_x = ridge(x * NY + y)

    @pl.loop(0, n_x)
    def _(j):
        got = wide(sum_x[j, pl.ds(pl.multiple_of(y * PIECE, PIECE), PIECE), :])
        for k in range(1, NY):
            got = got + wide(second_x[y_peer(k), j])
        stat[j] = (got + ridge_x).astype(BF16)

    @pl.loop(0, NX * NY)
    def _(k):
        o = lax.rem(me + k, NX * NY)
        for s in range(CAP):
            a2a_send[o, s] = stat[slot_idx[o * CAP + s]]

        @pl.when(k > 0)
        def _():
            send(A2A, a2a_send.at[o], pieces_out.at[me], {"dp": o, "blocks": col})

    mine = pltpu.make_async_copy(a2a_send.at[me], pieces_out.at[me], sems.at[0, OWN])
    mine.start()

    whole(E2, eybuf.at[pl.ds(0, NY - 1)]).wait_recv()
    diag_out[...] = eybuf[0] + eybuf[1] + eybuf[2] + eybuf[3]

    if nz > 1:
        whole(Z, zbuf.at[pl.ds(0, nz - 1)]).wait_send()
    whole(C, c_like).wait_send()
    whole(X1, first_x.at[pl.ds(0, NX - 1)]).wait_send()
    whole(X2, second_x.at[pl.ds(0, NY - 1)]).wait_send()
    if n_y:
        whole(Y1, first_y.at[pl.ds(0, NY - 1)]).wait_send()
        whole(Y2, second_y.at[pl.ds(0, NX - 1)]).wait_send()
    whole(E1, ebuf.at[pl.ds(0, NX - 1)]).wait_send()
    whole(E2, eybuf.at[pl.ds(0, NY - 1)]).wait_send()
    whole(A2A, a2a_send.at[pl.ds(0, NX * NY - 1)]).wait_recv()
    whole(A2A, a2a_send.at[pl.ds(0, NX * NY - 1)]).wait_send()
    mine.wait()


def product(left, right):
    return lax.dot_general(left, right, (((1,), (0,)), ((), ())), preferred_element_type=F32)


def newton_kernel(count, owner_ref, index_ref, pieces_ref, diag_ref, out_ref, mat):
    order = mat.shape[-1]
    me = index_ref[0]
    rows = lax.broadcasted_iota(jnp.int32, (T, T), 0)
    cols = lax.broadcasted_iota(jnp.int32, (T, T), 1)
    unit5 = jnp.where(
        lax.broadcasted_iota(jnp.int32, (order, order), 0) == lax.broadcasted_iota(jnp.int32, (order, order), 1), 5.0, 0.0
    ).astype(F32)
    for s in range(CAP):
        found = jnp.int32(0)
        seen = jnp.int32(0)
        for j in range(count):
            hit = owner_ref[j] == me
            found = jnp.where(jnp.logical_and(hit, seen == s), j, found)
            seen = seen + jnp.where(hit, 1, 0)
        live = seen > s

        x_first = found < X_FIRST

        def tile(t):
            halves = []
            for p in (2 * t, 2 * t + 1):
                halves.append(pieces_ref[jnp.where(x_first, p, p % NX * NY + p // NX), s])
            return jnp.concatenate(halves, axis=0).astype(F32)

        def put(r, k, value):
            mat[s, r * T:(r + 1) * T, k * T:(k + 1) * T] = value

        for t, (r, k) in enumerate(((2, 0), (2, 1), (3, 0), (3, 1), (1, 0), (3, 2))):
            value = tile(t)
            put(r, k, value)
            put(k, r, value.T)
        for h in range(2):
            value = tile(6 + h)
            turned = value.T
            edge = (diag_ref[pl.ds(2 * found + h, 1), :] + RIDGE).astype(BF16).astype(F32)
            put(2 * h, 2 * h, jnp.where(rows >= cols, value, turned))
            put(2 * h + 1, 2 * h + 1, jnp.where(rows < cols, value, jnp.where(rows == cols, edge, turned)))
        full = mat[s]
        z = 0.5 * order**0.5 * lax.rsqrt(jnp.sum(full * full, axis=(0, 1), keepdims=True) + 1e-06)
        coupled = z * full
        factor = ((unit5 - coupled) * 0.25).astype(BF16)
        iterate = (jnp.sqrt(jnp.sqrt(z)) * factor.astype(F32)).astype(BF16)
        square = product(factor, factor).astype(BF16)
        fourth = product(square, square).astype(BF16)
        coupled = product(fourth, coupled.astype(BF16))
        factor = ((unit5 - coupled) * 0.25).astype(BF16)
        root = product(iterate, factor)
        out_ref[s] = jnp.where(live, root, 0.0).astype(BF16)


def body(n_blocks, grads, owner):
    count, order = grads.shape[1], grads.shape[2]
    entries = n_blocks * count * order * order
    n = NX * NY
    n_x = min(X_FIRST, count)
    n_y = max(count - n_x, 1)
    nz = n_blocks // NC
    dma = pltpu.SemaphoreType.DMA
    vmem = pltpu.VMEM
    pieces, diag = pl.pallas_call(
        functools.partial(exchange_kernel, n_blocks, count, float(entries)),
        out_shape=(
            jax.ShapeDtypeStruct((n, CAP, PIECE, T), BF16),
            jax.ShapeDtypeStruct((16, T), F32),
        ),
        in_specs=[pl.BlockSpec(memory_space=pltpu.SMEM), pl.BlockSpec(memory_space=pl.ANY)],
        out_specs=(pl.BlockSpec(memory_space=pl.ANY), pl.BlockSpec(memory_space=pltpu.VMEM)),
        scratch_shapes=[
            vmem((count, order, order), BF16),
            vmem((count, NX, QUARTER, T), BF16),
            vmem((NX, n_x, QUARTER, T), BF16),
            vmem((NY, n_y, QUARTER, T), BF16),
            vmem((n_x, QUARTER, T), BF16),
            vmem((n_y, QUARTER, T), BF16),
            vmem((NY, n_x, PIECE, T), BF16),
            vmem((NX, n_y, PIECE, T), BF16),
            vmem((count + 1, PIECE, T), BF16),
            vmem((n, CAP, PIECE, T), BF16),
            vmem((nz, 8, T), F32),
            vmem(((NX + NY) * NC, 8, T), F32),
            vmem((NX + NY, T), F32),
            vmem((NX, 16, T), F32),
            vmem((NY, 16, T), F32),
            pltpu.SMEM((n * CAP,), jnp.int32),
            dma((count,)),
            dma((2, 10)),
        ],
        compiler_params=pltpu.CompilerParams(
            collective_id=0, has_side_effects=True, vmem_limit_bytes=61 * 1024 * 1024
        ),
        cost_estimate=pl.CostEstimate(flops=2 * count * order**3, bytes_accessed=grads.size * 2, transcendentals=0),
        name="exchange",
    )(owner[:, 0], grads)
    index = lax.axis_index("dp").reshape(1).astype(jnp.int32)
    roots = pl.pallas_call(
        functools.partial(newton_kernel, count),
        out_shape=jax.ShapeDtypeStruct((CAP, order, order), BF16),
        in_specs=[
            pl.BlockSpec(memory_space=pltpu.SMEM),
            pl.BlockSpec(memory_space=pltpu.SMEM),
            pl.BlockSpec(memory_space=pltpu.VMEM),
            pl.BlockSpec(memory_space=pltpu.VMEM),
        ],
        out_specs=pl.BlockSpec(memory_space=pltpu.VMEM),
        scratch_shapes=[vmem((CAP, order, order), F32)],
        compiler_params=pltpu.CompilerParams(vmem_limit_bytes=32 * 1024 * 1024),
        cost_estimate=pl.CostEstimate(flops=16 * order**3, bytes_accessed=4 * order * order, transcendentals=0),
        name="newton",
    )(owner[:, 0], index, pieces, diag)
    return roots[None, None]


def solution(mesh):
    return jax.shard_map(
        functools.partial(body, mesh.shape["blocks"]),
        mesh=mesh,
        in_specs=(P("dp", "blocks", None, None), P("blocks", None)),
        out_specs=P("blocks", "dp", None, None, None),
        check_vma=False,
    )
```

```python
import functools

import jax
import jax.numpy as jnp
from jax import lax
from jax.experimental import pallas as pl
from jax.experimental.pallas import tpu as pltpu
from jax.sharding import PartitionSpec as P

CAP = 2
CLIP = 0.25
RIDGE = 0.02
T = 128
QUARTER = 256
PIECE = 64
NX = 4
NY = 4
NC = 4
Y_FIRST = 2
EARLY = 4
MESH = pl.DeviceIdType.MESH
F32 = jnp.float32
BF16 = jnp.bfloat16


def gram(left, right):
    return lax.dot_general(left, right, (((1,), (1,)), ((), ())), preferred_element_type=F32)


def product(left, right):
    return lax.dot_general(left, right, (((1,), (0,)), ((), ())), preferred_element_type=F32)


def exchange_kernel(
    n_blocks, count, entries,
    owner_hbm, grads_ref, out_ref,
    g_buf, packed, first_x, first_y, sum_x, sum_y, second_x, second_y, stat, a2a_send, pieces, mat, roots,
    zbuf, cbuf, wbuf, ebuf, eybuf, owner_ref, slot_idx,
    g_sem, sems,
):
    nz = n_blocks // NC
    order = g_buf.shape[-1]
    n_y = min(Y_FIRST, count - 1)
    n_x = count - n_y
    me = lax.axis_index("dp")
    col = lax.axis_index("blocks")
    x, y = me // NY, me % NY
    z, c = col // NC, col % NC

    def device(xx, yy, zz, cc):
        return {"dp": xx * NY + yy, "blocks": zz * NC + cc}

    def x_peer(k):
        return lax.rem(x + k, NX)

    def y_peer(k):
        return lax.rem(y + k, NY)

    def c_peer(k):
        return lax.rem(c + k, NC)

    Z, C, X1, Y1, X2, Y2, E1, E2, OWN, A2A = range(10)

    def send(group, src, dst, dev):
        pltpu.make_async_remote_copy(
            src_ref=src, dst_ref=dst, send_sem=sems.at[0, group], recv_sem=sems.at[1, group],
            device_id=dev, device_id_type=MESH,
        ).start()

    def whole(group, like):
        return pltpu.make_async_remote_copy(
            src_ref=like, dst_ref=like, send_sem=sems.at[0, group], recv_sem=sems.at[1, group],
            device_id=device(x_peer(1), y, z, c), device_id_type=MESH,
        )

    def load(j):
        return pltpu.make_async_copy(grads_ref.at[0, j], g_buf.at[j], g_sem.at[j])

    barrier = pltpu.get_barrier_semaphore()

    def greet(dev):
        pl.semaphore_signal(barrier, inc=1, device_id=dev, device_id_type=MESH)

    def z_peers(act):
        if nz > 1:
            @pl.loop(1, nz)
            def _(k):
                act(lax.rem(z + k, nz))

    def plane_peers(act):
        @pl.loop(1, NX * NY)
        def _(k):
            act(lax.rem(me + k, NX * NY))

    def weight_peers(act, own_c):
        @pl.loop(0 if own_c else 1, NC)
        def _(k):
            @pl.loop(1, NX)
            def _(i):
                act(device(x_peer(i), y, z, c_peer(k)), 0)
                act(device(x, y_peer(i), z, c_peer(k)), 1)

        @pl.loop(1, NC)
        def _(k):
            act(device(x, y, z, c_peer(k)), 0)

    z_peers(lambda p: greet(device(x, y, p, c)))
    for j in range(count):
        load(j).start()
    owners = pltpu.make_async_copy(owner_hbm, owner_ref, sems.at[1, OWN])
    owners.start()
    weight_peers(lambda dev, axis: greet(dev), False)
    plane_peers(lambda p: greet({"dp": p, "blocks": col}))

    mine_x, mine_y = x * NC + c, (NX + y) * NC + c
    cbuf[mine_x] = jnp.zeros((8, T), F32)

    @pl.loop(0, count)
    def _(j):
        load(j).wait()
        values = g_buf[j].astype(F32)
        squares = jnp.sum((values * values).reshape(order // 8, 8, order), axis=0)
        part = squares[:, :T]
        for k in range(T, order, T):
            part = part + squares[:, k:k + T]
        cbuf[mine_x] += part

    rows = lax.broadcasted_iota(jnp.int32, (T, T), 0)
    cols = lax.broadcasted_iota(jnp.int32, (T, T), 1)
    lower = rows >= cols
    eye = rows == cols
    ebuf[x] = jnp.zeros((16, T), F32)

    def outer(j):
        top, bottom = g_buf[j, :256], g_buf[j, 256:]
        cross = gram(bottom, top)
        for t, (r, k) in enumerate(((0, 0), (0, 1), (1, 0), (1, 1))):
            packed[j, t // 2, (t % 2) * T:(t % 2 + 1) * T, :] = cross[
                r * T:(r + 1) * T, k * T:(k + 1) * T
            ].astype(BF16)
        for h, part in enumerate((top, bottom)):
            own = gram(part, part)
            d0, d1 = own[:T, :T], own[T:, T:]
            packed[j, 2, h * T:(h + 1) * T, :] = own[T:, :T].astype(BF16)
            packed[j, 3, h * T:(h + 1) * T, :] = jnp.where(lower, d0, d1).astype(BF16)
            ebuf[x, pl.ds(2 * j + h, 1), :] = jnp.sum(jnp.where(eye, d1, 0.0), axis=0, keepdims=True)

    def first_sends(j):
        @pl.when(j >= n_y)
        def _():
            @pl.loop(1, NX)
            def _(k):
                to = x_peer(k)
                send(X1, packed.at[j, to], first_x.at[x, j - n_y], device(to, y, z, c))

        if n_y:
            @pl.when(j < n_y)
            def _():
                @pl.loop(1, NY)
                def _(k):
                    to = y_peer(k)
                    send(Y1, packed.at[j, to], first_y.at[y, j], device(x, to, z, c))

    early = min(EARLY, count)
    pl.loop(0, early)(outer)

    pl.semaphore_wait(barrier, NX * NY - 1 + nz - 1 + (NX + NY - 1) * (NC - 1))

    def send_sum(dev, axis):
        send(C, cbuf.at[mine_x], cbuf.at[mine_x if axis == 0 else mine_y], dev)

    weight_peers(send_sum, True)
    c_like = cbuf.at[pl.ds(0, NX * NC - 1 + (NY - 1) * NC)]

    pl.loop(0, early)(first_sends)

    @pl.loop(early, count)
    def _(j):
        outer(j)
        first_sends(j)

    @pl.loop(1, NX)
    def _(k):
        send(E1, ebuf.at[x], ebuf.at[x], device(x_peer(k), y, z, c))

    whole(C, c_like).wait_recv()
    cbuf[mine_y] = cbuf[mine_x]
    sums = [jnp.sum(jnp.sum(cbuf[k * NC:(k + 1) * NC], axis=0), axis=0, keepdims=True) for k in range(NX + NY)]
    zbuf[z] = jnp.concatenate(sums, axis=0)
    z_peers(lambda p: send(Z, zbuf.at[z], zbuf.at[z], device(x, y, p, c)))

    owners.wait()

    @pl.loop(0, NX * NY * CAP)
    def _(i):
        target, slot = i // CAP, i % CAP
        found = jnp.int32(count)
        seen = jnp.int32(0)
        for j in range(count):
            hit = owner_ref[j] == target
            found = jnp.where(jnp.logical_and(hit, seen == slot), j, found)
            seen = seen + jnp.where(hit, 1, 0)
        slot_idx[i] = found

    stat[count] = jnp.zeros((PIECE, T), BF16)

    if nz > 1:
        whole(Z, zbuf.at[pl.ds(0, nz - 1)]).wait_recv()
    sums = jnp.sum(jnp.sum(zbuf[...], axis=0), axis=1, keepdims=True)
    scale = jnp.minimum(1.0, CLIP * lax.rsqrt(jnp.broadcast_to(sums, (NX + NY, T)) / entries + 1e-06))
    wbuf[...] = scale * scale / (NX * NY * order)

    def weight_x(k):
        return wbuf[pl.ds(k, 1), :]

    def weight_y(k):
        return wbuf[pl.ds(NX + k, 1), :]

    def wide(value):
        return value.astype(F32)

    whole(X1, first_x.at[pl.ds(0, NX - 1)]).wait_recv()

    @pl.loop(0, n_x)
    def _(j):
        got = weight_x(x) * wide(packed[n_y + j, x])
        for k in range(1, NX):
            got = got + weight_x(x_peer(k)) * wide(first_x[x_peer(k), j])
        sum_x[j] = got.astype(BF16)

    for k in range(1, NY):
        to = y_peer(k)
        piece = pl.ds(pl.multiple_of(to * PIECE, PIECE), PIECE)
        send(X2, sum_x.at[:, piece], second_x.at[y], device(x, to, z, c))

    if n_y:
        whole(Y1, first_y.at[pl.ds(0, NY - 1)]).wait_recv()

        @pl.loop(0, n_y)
        def _(j):
            got = weight_x(x) * wide(packed[j, y])
            for k in range(1, NY):
                got = got + weight_y(y_peer(k)) * wide(first_y[y_peer(k), j])
            sum_y[j] = got.astype(BF16)

        for k in range(1, NX):
            to = x_peer(k)
            piece = pl.ds(pl.multiple_of(to * PIECE, PIECE), PIECE)
            send(Y2, sum_y.at[:, piece], second_y.at[x], device(to, y, z, c))

    whole(E1, ebuf.at[pl.ds(0, NX - 1)]).wait_recv()
    diag = jnp.zeros((16, T), F32)
    for k in range(NX):
        diag = diag + wbuf[k:k + 1, :] * ebuf[k]
    eybuf[y] = diag

    @pl.loop(1, NY)
    def _(k):
        send(E2, eybuf.at[y], eybuf.at[y], device(x, y_peer(k), z, c))

    lane = lax.broadcasted_iota(jnp.int32, (PIECE, T), 1)
    row = lax.broadcasted_iota(jnp.int32, (PIECE, T), 0)

    def ridge(position):
        packed_row = position * PIECE + row
        on_diagonal = jnp.logical_and(packed_row >= 6 * T, packed_row % T == lane)
        return jnp.where(on_diagonal, RIDGE, 0.0).astype(F32)

    if n_y:
        whole(Y2, second_y.at[pl.ds(0, NX - 1)]).wait_recv()
        ridge_y = ridge(y * NX + x)

        @pl.loop(0, n_y)
        def _(j):
            got = wide(sum_y[j, pl.ds(pl.multiple_of(x * PIECE, PIECE), PIECE), :])
            for k in range(1, NX):
                got = got + wide(second_y[x_peer(k), j])
            stat[j] = (got + ridge_y).astype(BF16)

    whole(X2, second_x.at[pl.ds(0, NY - 1)]).wait_recv()
    ridge_x = ridge(x * NY + y)

    @pl.loop(0, n_x)
    def _(j):
        got = wide(sum_x[j, pl.ds(pl.multiple_of(y * PIECE, PIECE), PIECE), :])
        for k in range(1, NY):
            got = got + wide(second_x[y_peer(k), j])
        stat[n_y + j] = (got + ridge_x).astype(BF16)

    @pl.loop(0, CAP)
    def _(s):
        @pl.loop(1, NX * NY)
        def _(k):
            o = lax.rem(me + k, NX * NY)
            a2a_send[s, o] = stat[slot_idx[o * CAP + s]]
            send(A2A + s, a2a_send.at[s, o], pieces.at[s, me], {"dp": o, "blocks": col})

        pieces[s, me] = stat[slot_idx[me * CAP + s]]

    whole(E2, eybuf.at[pl.ds(0, NY - 1)]).wait_recv()
    diagonal = eybuf[0] + eybuf[1] + eybuf[2] + eybuf[3] + RIDGE
    diagonal_row = lax.broadcasted_iota(jnp.int32, (16, T), 0)
    unit5 = jnp.where(
        lax.broadcasted_iota(jnp.int32, (order, order), 0) == lax.broadcasted_iota(jnp.int32, (order, order), 1), 5.0, 0.0
    ).astype(F32)

    @pl.loop(0, CAP)
    def _(s):
        block = slot_idx[me * CAP + s]
        x_first = block >= n_y
        whole(A2A + s, a2a_send.at[0, pl.ds(0, NX * NY - 1)]).wait_recv()

        def tile(t):
            halves = []
            for p in (2 * t, 2 * t + 1):
                halves.append(jnp.where(x_first, wide(pieces[s, p]), wide(pieces[s, p % NX * NY + p // NX])))
            return jnp.concatenate(halves, axis=0)

        def put(r, k, value):
            mat[r * T:(r + 1) * T, k * T:(k + 1) * T] = value

        for t, (r, k) in enumerate(((2, 0), (2, 1), (3, 0), (3, 1), (1, 0), (3, 2))):
            value = tile(t)
            put(r, k, value)
            put(k, r, value.T)
        for h in range(2):
            value = tile(6 + h)
            turned = value.T
            edge = jnp.sum(jnp.where(diagonal_row == 2 * block + h, diagonal, 0.0), axis=0, keepdims=True)
            edge = wide(edge.astype(BF16))
            put(2 * h, 2 * h, jnp.where(lower, value, turned))
            put(2 * h + 1, 2 * h + 1, jnp.where(rows < cols, value, jnp.where(eye, edge, turned)))
        full = mat[...]
        z0 = 0.5 * order**0.5 * lax.rsqrt(jnp.sum(full * full, axis=(0, 1), keepdims=True) + 1e-06)
        coupled = z0 * full
        factor = ((unit5 - coupled) * 0.25).astype(BF16)
        iterate = (jnp.sqrt(jnp.sqrt(z0)) * wide(factor)).astype(BF16)
        square = product(factor, factor).astype(BF16)
        fourth = product(square, square).astype(BF16)
        coupled = product(fourth, coupled.astype(BF16))
        factor = ((unit5 - coupled) * 0.25).astype(BF16)
        root = product(iterate, factor)
        roots[s] = jnp.where(block < count, root, 0.0).astype(BF16)
        pltpu.make_async_copy(roots.at[s], out_ref.at[s], sems.at[0, OWN]).start()

    if nz > 1:
        whole(Z, zbuf.at[pl.ds(0, nz - 1)]).wait_send()
    whole(C, c_like).wait_send()
    whole(X1, first_x.at[pl.ds(0, NX - 1)]).wait_send()
    whole(X2, second_x.at[pl.ds(0, NY - 1)]).wait_send()
    if n_y:
        whole(Y1, first_y.at[pl.ds(0, NY - 1)]).wait_send()
        whole(Y2, second_y.at[pl.ds(0, NX - 1)]).wait_send()
    whole(E1, ebuf.at[pl.ds(0, NX - 1)]).wait_send()
    whole(E2, eybuf.at[pl.ds(0, NY - 1)]).wait_send()
    for s in range(CAP):
        whole(A2A + s, a2a_send.at[0, pl.ds(0, NX * NY - 1)]).wait_send()
    pltpu.make_async_copy(roots, out_ref, sems.at[0, OWN]).wait()


def finish_kernel(roots_ref, out_ref, sem):
    copy = pltpu.make_async_copy(roots_ref, out_ref, sem)
    copy.start()
    copy.wait()


def body(n_blocks, grads, owner):
    count, order = grads.shape[1], grads.shape[2]
    entries = n_blocks * count * order * order
    n = NX * NY
    n_y = min(Y_FIRST, count - 1)
    n_x = count - n_y
    nz = n_blocks // NC
    dma = pltpu.SemaphoreType.DMA
    vmem = pltpu.VMEM
    roots = pl.pallas_call(
        functools.partial(exchange_kernel, n_blocks, count, float(entries)),
        out_shape=jax.ShapeDtypeStruct((CAP, order, order), BF16),
        in_specs=[pl.BlockSpec(memory_space=pl.ANY), pl.BlockSpec(memory_space=pl.ANY)],
        out_specs=pl.BlockSpec(memory_space=pl.ANY),
        scratch_shapes=[
            vmem((count, order, order), BF16),
            vmem((count, NX, QUARTER, T), BF16),
            vmem((NX, n_x, QUARTER, T), BF16),
            vmem((NY, max(n_y, 1), QUARTER, T), BF16),
            vmem((n_x, QUARTER, T), BF16),
            vmem((max(n_y, 1), QUARTER, T), BF16),
            vmem((NY, n_x, PIECE, T), BF16),
            vmem((NX, max(n_y, 1), PIECE, T), BF16),
            vmem((count + 1, PIECE, T), BF16),
            vmem((CAP, n, PIECE, T), BF16),
            vmem((CAP, n, PIECE, T), BF16),
            vmem((order, order), F32),
            vmem((CAP, order, order), BF16),
            vmem((nz, 8, T), F32),
            vmem(((NX + NY) * NC, 8, T), F32),
            vmem((NX + NY, T), F32),
            vmem((NX, 16, T), F32),
            vmem((NY, 16, T), F32),
            pltpu.SMEM((count,), jnp.int32),
            pltpu.SMEM((n * CAP,), jnp.int32),
            dma((count,)),
            dma((2, 9 + CAP)),
        ],
        compiler_params=pltpu.CompilerParams(
            collective_id=0, has_side_effects=True, vmem_limit_bytes=61 * 1024 * 1024
        ),
        cost_estimate=pl.CostEstimate(
            flops=2 * count * order**3 + 16 * order**3, bytes_accessed=grads.size * 2, transcendentals=0
        ),
        name="exchange",
    )(owner[:, 0], grads)
    out = pl.pallas_call(
        finish_kernel,
        out_shape=jax.ShapeDtypeStruct((CAP, order, order), BF16),
        in_specs=[pl.BlockSpec(memory_space=pl.ANY)],
        out_specs=pl.BlockSpec(memory_space=pl.ANY),
        scratch_shapes=[dma(())],
        cost_estimate=pl.CostEstimate(flops=0, bytes_accessed=4 * CAP * order * order, transcendentals=0),
        compiler_params=pltpu.CompilerParams(vmem_limit_bytes=63 * 1024 * 1024),
        name="finish",
    )(roots)
    return out[None, None]


def solution(mesh):
    return jax.shard_map(
        functools.partial(body, mesh.shape["blocks"]),
        mesh=mesh,
        in_specs=(P("dp", "blocks", None, None), P("blocks", None)),
        out_specs=P("blocks", "dp", None, None, None),
        check_vma=False,
    )
```

```python
import functools

import jax
import jax.numpy as jnp
from jax import lax
from jax.experimental import pallas as pl
from jax.experimental.pallas import tpu as pltpu
from jax.sharding import PartitionSpec as P

CAP = 2
CLIP = 0.25
RIDGE = 0.02
T = 128
QUARTER = 256
PIECE = 64
NX = 4
NY = 4
NC = 4
Y_FIRST = 2
EARLY = 4
MESH = pl.DeviceIdType.MESH
F32 = jnp.float32
BF16 = jnp.bfloat16


def gram(left, right):
    return lax.dot_general(left, right, (((1,), (1,)), ((), ())), preferred_element_type=F32)


def product(left, right):
    return lax.dot_general(left, right, (((1,), (0,)), ((), ())), preferred_element_type=F32)


def exchange_kernel(
    n_blocks, count, entries,
    owner_hbm, grads_ref, out_ref,
    g_buf, packed, first_x, first_y, sum_x, sum_y, second_x, second_y, stat, a2a_send, pieces, mat, roots,
    zbuf, cbuf, wbuf, ebuf, eybuf, owner_ref, slot_idx,
    g_sem, sems,
):
    nz = n_blocks // NC
    order = g_buf.shape[-1]
    n_y = min(Y_FIRST, count - 1)
    n_x = count - n_y
    me = lax.axis_index("dp")
    col = lax.axis_index("blocks")
    x, y = me // NY, me % NY
    z, c = col // NC, col % NC

    def device(xx, yy, zz, cc):
        return {"dp": xx * NY + yy, "blocks": zz * NC + cc}

    def x_peer(k):
        return lax.rem(x + k, NX)

    def y_peer(k):
        return lax.rem(y + k, NY)

    def c_peer(k):
        return lax.rem(c + k, NC)

    Z, C, X1, Y1, X2, Y2, E1, E2, OWN, A2A = range(10)

    def send(group, src, dst, dev):
        pltpu.make_async_remote_copy(
            src_ref=src, dst_ref=dst, send_sem=sems.at[0, group], recv_sem=sems.at[1, group],
            device_id=dev, device_id_type=MESH,
        ).start()

    def whole(group, like):
        return pltpu.make_async_remote_copy(
            src_ref=like, dst_ref=like, send_sem=sems.at[0, group], recv_sem=sems.at[1, group],
            device_id=device(x_peer(1), y, z, c), device_id_type=MESH,
        )

    def load(j):
        return pltpu.make_async_copy(grads_ref.at[0, j], g_buf.at[j], g_sem.at[j])

    barrier = pltpu.get_barrier_semaphore()

    def greet(dev):
        pl.semaphore_signal(barrier, inc=1, device_id=dev, device_id_type=MESH)

    def z_peers(act):
        if nz > 1:
            @pl.loop(1, nz)
            def _(k):
                act(lax.rem(z + k, nz))

    def plane_peers(act):
        @pl.loop(1, NX * NY)
        def _(k):
            act(lax.rem(me + k, NX * NY))

    def weight_peers(act, own_c):
        @pl.loop(0 if own_c else 1, NC)
        def _(k):
            @pl.loop(1, NX)
            def _(i):
                act(device(x_peer(i), y, z, c_peer(k)), 0)
                act(device(x, y_peer(i), z, c_peer(k)), 1)

        @pl.loop(1, NC)
        def _(k):
            act(device(x, y, z, c_peer(k)), 0)

    z_peers(lambda p: greet(device(x, y, p, c)))
    for j in range(count):
        load(j).start()
    owners = pltpu.make_async_copy(owner_hbm, owner_ref, sems.at[1, OWN])
    owners.start()
    weight_peers(lambda dev, axis: greet(dev), False)
    plane_peers(lambda p: greet({"dp": p, "blocks": col}))

    mine_x, mine_y = x * NC + c, (NX + y) * NC + c
    cbuf[mine_x] = jnp.zeros((8, T), F32)

    @pl.loop(0, count)
    def _(j):
        load(j).wait()
        values = g_buf[j].astype(F32)
        squares = jnp.sum((values * values).reshape(order // 8, 8, order), axis=0)
        part = squares[:, :T]
        for k in range(T, order, T):
            part = part + squares[:, k:k + T]
        cbuf[mine_x] += part

    rows = lax.broadcasted_iota(jnp.int32, (T, T), 0)
    cols = lax.broadcasted_iota(jnp.int32, (T, T), 1)
    lower = rows >= cols
    eye = rows == cols
    ebuf[x] = jnp.zeros((16, T), F32)

    def outer(j):
        top, bottom = g_buf[j, :256], g_buf[j, 256:]
        cross = gram(bottom, top)
        for t, (r, k) in enumerate(((0, 0), (0, 1), (1, 0), (1, 1))):
            packed[j, t // 2, (t % 2) * T:(t % 2 + 1) * T, :] = cross[
                r * T:(r + 1) * T, k * T:(k + 1) * T
            ].astype(BF16)
        for h, part in enumerate((top, bottom)):
            own = gram(part, part)
            d0, d1 = own[:T, :T], own[T:, T:]
            packed[j, 2, h * T:(h + 1) * T, :] = own[T:, :T].astype(BF16)
            packed[j, 3, h * T:(h + 1) * T, :] = jnp.where(lower, d0, d1).astype(BF16)
            ebuf[x, pl.ds(2 * j + h, 1), :] = jnp.sum(jnp.where(eye, d1, 0.0), axis=0, keepdims=True)

    def first_sends(j):
        @pl.when(j >= n_y)
        def _():
            @pl.loop(1, NX)
            def _(k):
                to = x_peer(k)
                send(X1, packed.at[j, to], first_x.at[x, j - n_y], device(to, y, z, c))

        if n_y:
            @pl.when(j < n_y)
            def _():
                @pl.loop(1, NY)
                def _(k):
                    to = y_peer(k)
                    send(Y1, packed.at[j, to], first_y.at[y, j], device(x, to, z, c))

    early = min(EARLY, count)
    pl.loop(0, early)(outer)

    pl.semaphore_wait(barrier, NX * NY - 1 + nz - 1 + (NX + NY - 1) * (NC - 1))

    def send_sum(dev, axis):
        send(C, cbuf.at[mine_x], cbuf.at[mine_x if axis == 0 else mine_y], dev)

    weight_peers(send_sum, True)
    c_like = cbuf.at[pl.ds(0, NX * NC - 1 + (NY - 1) * NC)]

    pl.loop(0, early)(first_sends)

    @pl.loop(early, count)
    def _(j):
        outer(j)
        first_sends(j)

    @pl.loop(1, NX)
    def _(k):
        send(E1, ebuf.at[x], ebuf.at[x], device(x_peer(k), y, z, c))

    whole(C, c_like).wait_recv()
    cbuf[mine_y] = cbuf[mine_x]
    sums = [jnp.sum(jnp.sum(cbuf[k * NC:(k + 1) * NC], axis=0), axis=0, keepdims=True) for k in range(NX + NY)]
    zbuf[z] = jnp.concatenate(sums, axis=0)
    z_peers(lambda p: send(Z, zbuf.at[z], zbuf.at[z], device(x, y, p, c)))

    owners.wait()

    @pl.loop(0, NX * NY * CAP)
    def _(i):
        target, slot = i // CAP, i % CAP
        found = jnp.int32(count)
        seen = jnp.int32(0)
        for j in range(count):
            hit = owner_ref[j] == target
            found = jnp.where(jnp.logical_and(hit, seen == slot), j, found)
            seen = seen + jnp.where(hit, 1, 0)
        slot_idx[i] = found

    stat[count] = jnp.zeros((PIECE, T), BF16)

    if nz > 1:
        whole(Z, zbuf.at[pl.ds(0, nz - 1)]).wait_recv()
    sums = jnp.sum(jnp.sum(zbuf[...], axis=0), axis=1, keepdims=True)
    scale = jnp.minimum(1.0, CLIP * lax.rsqrt(jnp.broadcast_to(sums, (NX + NY, T)) / entries + 1e-06))
    wbuf[...] = scale * scale / (NX * NY * order)

    def weight_x(k):
        return wbuf[pl.ds(k, 1), :]

    def weight_y(k):
        return wbuf[pl.ds(NX + k, 1), :]

    def wide(value):
        return value.astype(F32)

    whole(X1, first_x.at[pl.ds(0, NX - 1)]).wait_recv()

    @pl.loop(0, n_x)
    def _(j):
        got = weight_x(x) * wide(packed[n_y + j, x])
        for k in range(1, NX):
            got = got + weight_x(x_peer(k)) * wide(first_x[x_peer(k), j])
        sum_x[j] = got.astype(BF16)

    for k in range(1, NY):
        to = y_peer(k)
        piece = pl.ds(pl.multiple_of(to * PIECE, PIECE), PIECE)
        send(X2, sum_x.at[:, piece], second_x.at[y], device(x, to, z, c))

    if n_y:
        whole(Y1, first_y.at[pl.ds(0, NY - 1)]).wait_recv()

        @pl.loop(0, n_y)
        def _(j):
            got = weight_x(x) * wide(packed[j, y])
            for k in range(1, NY):
                got = got + weight_y(y_peer(k)) * wide(first_y[y_peer(k), j])
            sum_y[j] = got.astype(BF16)

        for k in range(1, NX):
            to = x_peer(k)
            piece = pl.ds(pl.multiple_of(to * PIECE, PIECE), PIECE)
            send(Y2, sum_y.at[:, piece], second_y.at[x], device(to, y, z, c))

    whole(E1, ebuf.at[pl.ds(0, NX - 1)]).wait_recv()
    diag = jnp.zeros((16, T), F32)
    for k in range(NX):
        diag = diag + wbuf[k:k + 1, :] * ebuf[k]
    eybuf[y] = diag

    @pl.loop(1, NY)
    def _(k):
        send(E2, eybuf.at[y], eybuf.at[y], device(x, y_peer(k), z, c))

    lane = lax.broadcasted_iota(jnp.int32, (PIECE, T), 1)
    row = lax.broadcasted_iota(jnp.int32, (PIECE, T), 0)

    def ridge(position):
        packed_row = position * PIECE + row
        on_diagonal = jnp.logical_and(packed_row >= 6 * T, packed_row % T == lane)
        return jnp.where(on_diagonal, RIDGE, 0.0).astype(F32)

    if n_y:
        whole(Y2, second_y.at[pl.ds(0, NX - 1)]).wait_recv()
        ridge_y = ridge(y * NX + x)

        @pl.loop(0, n_y)
        def _(j):
            got = wide(sum_y[j, pl.ds(pl.multiple_of(x * PIECE, PIECE), PIECE), :])
            for k in range(1, NX):
                got = got + wide(second_y[x_peer(k), j])
            stat[j] = (got + ridge_y).astype(BF16)

    whole(X2, second_x.at[pl.ds(0, NY - 1)]).wait_recv()
    ridge_x = ridge(x * NY + y)

    @pl.loop(0, n_x)
    def _(j):
        got = wide(sum_x[j, pl.ds(pl.multiple_of(y * PIECE, PIECE), PIECE), :])
        for k in range(1, NY):
            got = got + wide(second_x[y_peer(k), j])
        stat[n_y + j] = (got + ridge_x).astype(BF16)

    @pl.loop(0, CAP)
    def _(s):
        @pl.loop(1, NX * NY)
        def _(k):
            o = lax.rem(me + k, NX * NY)
            a2a_send[s, o] = stat[slot_idx[o * CAP + s]]
            send(A2A + s, a2a_send.at[s, o], pieces.at[s, me], {"dp": o, "blocks": col})

        pieces[s, me] = stat[slot_idx[me * CAP + s]]

    whole(E2, eybuf.at[pl.ds(0, NY - 1)]).wait_recv()
    diagonal = eybuf[0] + eybuf[1] + eybuf[2] + eybuf[3] + RIDGE
    diagonal_row = lax.broadcasted_iota(jnp.int32, (16, T), 0)
    unit5 = jnp.where(
        lax.broadcasted_iota(jnp.int32, (order, order), 0) == lax.broadcasted_iota(jnp.int32, (order, order), 1), 5.0, 0.0
    ).astype(F32)

    @pl.loop(0, CAP)
    def _(s):
        block = slot_idx[me * CAP + s]
        x_first = block >= n_y
        whole(A2A + s, a2a_send.at[0, pl.ds(0, NX * NY - 1)]).wait_recv()

        def tile(t):
            halves = []
            for p in (2 * t, 2 * t + 1):
                halves.append(jnp.where(x_first, wide(pieces[s, p]), wide(pieces[s, p % NX * NY + p // NX])))
            return jnp.concatenate(halves, axis=0)

        def put(r, k, value):
            mat[r * T:(r + 1) * T, k * T:(k + 1) * T] = value

        for t, (r, k) in enumerate(((2, 0), (2, 1), (3, 0), (3, 1), (1, 0), (3, 2))):
            value = tile(t)
            put(r, k, value)
            put(k, r, value.T)
        for h in range(2):
            value = tile(6 + h)
            turned = value.T
            edge = jnp.sum(jnp.where(diagonal_row == 2 * block + h, diagonal, 0.0), axis=0, keepdims=True)
            edge = wide(edge.astype(BF16))
            put(2 * h, 2 * h, jnp.where(lower, value, turned))
            put(2 * h + 1, 2 * h + 1, jnp.where(rows < cols, value, jnp.where(eye, edge, turned)))
        full = mat[...]
        z0 = 0.5 * order**0.5 * lax.rsqrt(jnp.sum(full * full, axis=(0, 1), keepdims=True) + 1e-06)
        coupled = z0 * full
        factor = ((unit5 - coupled) * 0.25).astype(BF16)
        iterate = (jnp.sqrt(jnp.sqrt(z0)) * wide(factor)).astype(BF16)
        square = product(factor, factor).astype(BF16)
        fourth = product(square, square).astype(BF16)
        coupled = product(fourth, coupled.astype(BF16))
        factor = ((unit5 - coupled) * 0.25).astype(BF16)
        root = product(iterate, factor)
        roots[s] = jnp.where(block < count, root, 0.0).astype(BF16)
        pltpu.make_async_copy(roots.at[s], out_ref.at[s], sems.at[0, OWN]).start()

    if nz > 1:
        whole(Z, zbuf.at[pl.ds(0, nz - 1)]).wait_send()
    whole(C, c_like).wait_send()
    whole(X1, first_x.at[pl.ds(0, NX - 1)]).wait_send()
    whole(X2, second_x.at[pl.ds(0, NY - 1)]).wait_send()
    if n_y:
        whole(Y1, first_y.at[pl.ds(0, NY - 1)]).wait_send()
        whole(Y2, second_y.at[pl.ds(0, NX - 1)]).wait_send()
    whole(E1, ebuf.at[pl.ds(0, NX - 1)]).wait_send()
    whole(E2, eybuf.at[pl.ds(0, NY - 1)]).wait_send()
    for s in range(CAP):
        whole(A2A + s, a2a_send.at[0, pl.ds(0, NX * NY - 1)]).wait_send()
    pltpu.make_async_copy(roots, out_ref, sems.at[0, OWN]).wait()


def body(n_blocks, grads, owner):
    count, order = grads.shape[1], grads.shape[2]
    entries = n_blocks * count * order * order
    n = NX * NY
    n_y = min(Y_FIRST, count - 1)
    n_x = count - n_y
    nz = n_blocks // NC
    dma = pltpu.SemaphoreType.DMA
    vmem = pltpu.VMEM
    roots = pl.pallas_call(
        functools.partial(exchange_kernel, n_blocks, count, float(entries)),
        out_shape=jax.ShapeDtypeStruct((CAP, order, order), BF16),
        in_specs=[pl.BlockSpec(memory_space=pl.ANY), pl.BlockSpec(memory_space=pl.ANY)],
        out_specs=pl.BlockSpec(memory_space=pl.ANY),
        scratch_shapes=[
            vmem((count, order, order), BF16),
            vmem((count, NX, QUARTER, T), BF16),
            vmem((NX, n_x, QUARTER, T), BF16),
            vmem((NY, max(n_y, 1), QUARTER, T), BF16),
            vmem((n_x, QUARTER, T), BF16),
            vmem((max(n_y, 1), QUARTER, T), BF16),
            vmem((NY, n_x, PIECE, T), BF16),
            vmem((NX, max(n_y, 1), PIECE, T), BF16),
            vmem((count + 1, PIECE, T), BF16),
            vmem((CAP, n, PIECE, T), BF16),
            vmem((CAP, n, PIECE, T), BF16),
            vmem((order, order), F32),
            vmem((CAP, order, order), BF16),
            vmem((nz, 8, T), F32),
            vmem(((NX + NY) * NC, 8, T), F32),
            vmem((NX + NY, T), F32),
            vmem((NX, 16, T), F32),
            vmem((NY, 16, T), F32),
            pltpu.SMEM((count,), jnp.int32),
            pltpu.SMEM((n * CAP,), jnp.int32),
            dma((count,)),
            dma((2, 9 + CAP)),
        ],
        compiler_params=pltpu.CompilerParams(
            collective_id=0, has_side_effects=True, vmem_limit_bytes=61 * 1024 * 1024
        ),
        cost_estimate=pl.CostEstimate(
            flops=2 * count * order**3 + 16 * order**3, bytes_accessed=grads.size * 2, transcendentals=0
        ),
        name="exchange",
    )(owner[:, 0], grads)
    return roots[None, None]


def solution(mesh):
    return jax.shard_map(
        functools.partial(body, mesh.shape["blocks"]),
        mesh=mesh,
        in_specs=(P("dp", "blocks", None, None), P("blocks", None)),
        out_specs=P("blocks", "dp", None, None, None),
        check_vma=False,
    )
```

```python
import functools

import jax
import jax.numpy as jnp
from jax import lax
from jax.experimental import pallas as pl
from jax.experimental.pallas import tpu as pltpu
from jax.sharding import PartitionSpec as P

CAP = 2
CLIP = 0.25
RIDGE = 0.02
T = 128
QUARTER = 256
PIECE = 64
NX = 4
NY = 4
NC = 4
Y_FIRST = 2
EARLY = 4
MESH = pl.DeviceIdType.MESH
F32 = jnp.float32
BF16 = jnp.bfloat16


def gram(left, right):
    return lax.dot_general(left, right, (((1,), (1,)), ((), ())), preferred_element_type=F32)


def product(left, right):
    return lax.dot_general(left, right, (((1,), (0,)), ((), ())), preferred_element_type=F32)


def exchange_kernel(
    n_blocks, count, entries,
    owner_hbm, grads_ref, out_ref,
    g_buf, packed, first_x, first_y, sum_x, sum_y, second_x, second_y, stat, a2a_send, pieces, mat, roots,
    zbuf, cbuf, wbuf, ebuf, eybuf, owner_ref, slot_idx,
    g_sem, sems,
):
    nz = n_blocks // NC
    order = g_buf.shape[-1]
    n_y = min(Y_FIRST, count - 1)
    n_x = count - n_y
    me = lax.axis_index("dp")
    col = lax.axis_index("blocks")
    x, y = me // NY, me % NY
    z, c = col // NC, col % NC

    def device(xx, yy, zz, cc):
        return {"dp": xx * NY + yy, "blocks": zz * NC + cc}

    def x_peer(k):
        return lax.rem(x + k, NX)

    def y_peer(k):
        return lax.rem(y + k, NY)

    def c_peer(k):
        return lax.rem(c + k, NC)

    Z, C, X1, Y1, X2, Y2, E1, E2, OWN, A2A = range(10)

    def send(group, src, dst, dev):
        pltpu.make_async_remote_copy(
            src_ref=src, dst_ref=dst, send_sem=sems.at[0, group], recv_sem=sems.at[1, group],
            device_id=dev, device_id_type=MESH,
        ).start()

    def whole(group, like):
        return pltpu.make_async_remote_copy(
            src_ref=like, dst_ref=like, send_sem=sems.at[0, group], recv_sem=sems.at[1, group],
            device_id=device(x_peer(1), y, z, c), device_id_type=MESH,
        )

    def load(j):
        return pltpu.make_async_copy(grads_ref.at[0, j], g_buf.at[j], g_sem.at[j])

    barrier = pltpu.get_barrier_semaphore()

    def greet(dev):
        pl.semaphore_signal(barrier, inc=1, device_id=dev, device_id_type=MESH)

    def z_peers(act):
        for k in range(1, nz):
            act(lax.rem(z + k, nz))

    def plane_peers(act):
        @pl.loop(1, NX * NY)
        def _(k):
            act(lax.rem(me + k, NX * NY))

    def weight_peers(act, own_c):
        for k in range(1, NC + 1 if own_c else NC):
            for i in range(1, NX):
                act(device(x_peer(i), y, z, c_peer(k)), 0)
                act(device(x, y_peer(i), z, c_peer(k)), 1)
        for k in range(1, NC):
            act(device(x, y, z, c_peer(k)), 0)

    z_peers(lambda p: greet(device(x, y, p, c)))
    for j in range(count):
        load(j).start()
    owners = pltpu.make_async_copy(owner_hbm, owner_ref, sems.at[1, OWN])
    owners.start()
    weight_peers(lambda dev, axis: greet(dev), False)
    plane_peers(lambda p: greet({"dp": p, "blocks": col}))

    mine_x, mine_y = x * NC + c, (NX + y) * NC + c
    cbuf[mine_x] = jnp.zeros((8, T), F32)

    @pl.loop(0, count)
    def _(j):
        load(j).wait()
        values = g_buf[j].astype(F32)
        squares = jnp.sum((values * values).reshape(order // 8, 8, order), axis=0)
        part = squares[:, :T]
        for k in range(T, order, T):
            part = part + squares[:, k:k + T]
        cbuf[mine_x] += part

    rows = lax.broadcasted_iota(jnp.int32, (T, T), 0)
    cols = lax.broadcasted_iota(jnp.int32, (T, T), 1)
    lower = rows >= cols
    eye = rows == cols
    ebuf[x] = jnp.zeros((16, T), F32)

    def outer(j):
        top, bottom = g_buf[j, :256], g_buf[j, 256:]
        cross = gram(bottom, top)
        for t, (r, k) in enumerate(((0, 0), (0, 1), (1, 0), (1, 1))):
            packed[j, t // 2, (t % 2) * T:(t % 2 + 1) * T, :] = cross[
                r * T:(r + 1) * T, k * T:(k + 1) * T
            ].astype(BF16)
        for h, part in enumerate((top, bottom)):
            own = gram(part, part)
            d0, d1 = own[:T, :T], own[T:, T:]
            packed[j, 2, h * T:(h + 1) * T, :] = own[T:, :T].astype(BF16)
            packed[j, 3, h * T:(h + 1) * T, :] = jnp.where(lower, d0, d1).astype(BF16)
            ebuf[x, pl.ds(2 * j + h, 1), :] = jnp.sum(jnp.where(eye, d1, 0.0), axis=0, keepdims=True)

    def first_sends(j):
        @pl.when(j >= n_y)
        def _():
            @pl.loop(1, NX)
            def _(k):
                to = x_peer(k)
                send(X1, packed.at[j, to], first_x.at[x, j - n_y], device(to, y, z, c))

        if n_y:
            @pl.when(j < n_y)
            def _():
                @pl.loop(1, NY)
                def _(k):
                    to = y_peer(k)
                    send(Y1, packed.at[j, to], first_y.at[y, j], device(x, to, z, c))

    early = min(EARLY, count)
    pl.loop(0, early)(outer)

    pl.semaphore_wait(barrier, NX * NY - 1 + nz - 1 + (NX + NY - 1) * (NC - 1))

    def send_sum(dev, axis):
        send(C, cbuf.at[mine_x], cbuf.at[mine_x if axis == 0 else mine_y], dev)

    weight_peers(send_sum, True)
    c_like = cbuf.at[pl.ds(0, NX * NC - 1 + (NY - 1) * NC)]

    pl.loop(0, early)(first_sends)

    @pl.loop(early, count)
    def _(j):
        outer(j)
        first_sends(j)

    @pl.loop(1, NX)
    def _(k):
        send(E1, ebuf.at[x], ebuf.at[x], device(x_peer(k), y, z, c))

    whole(C, c_like).wait_recv()
    cbuf[mine_y] = cbuf[mine_x]
    sums = [jnp.sum(jnp.sum(cbuf[k * NC:(k + 1) * NC], axis=0), axis=0, keepdims=True) for k in range(NX + NY)]
    zbuf[z] = jnp.concatenate(sums, axis=0)
    z_peers(lambda p: send(Z, zbuf.at[z], zbuf.at[z], device(x, y, p, c)))

    owners.wait()

    @pl.loop(0, NX * NY * CAP)
    def _(i):
        target, slot = i // CAP, i % CAP
        found = jnp.int32(count)
        seen = jnp.int32(0)
        for j in range(count):
            hit = owner_ref[j] == target
            found = jnp.where(jnp.logical_and(hit, seen == slot), j, found)
            seen = seen + jnp.where(hit, 1, 0)
        slot_idx[i] = found

    stat[count] = jnp.zeros((PIECE, T), BF16)

    if nz > 1:
        whole(Z, zbuf.at[pl.ds(0, nz - 1)]).wait_recv()
    sums = jnp.sum(jnp.sum(zbuf[...], axis=0), axis=1, keepdims=True)
    scale = jnp.minimum(1.0, CLIP * lax.rsqrt(jnp.broadcast_to(sums, (NX + NY, T)) / entries + 1e-06))
    wbuf[...] = scale * scale / (NX * NY * order)

    def weight_x(k):
        return wbuf[pl.ds(k, 1), :]

    def weight_y(k):
        return wbuf[pl.ds(NX + k, 1), :]

    def wide(value):
        return value.astype(F32)

    whole(X1, first_x.at[pl.ds(0, NX - 1)]).wait_recv()

    @pl.loop(0, n_x, unroll=n_x)
    def _(j):
        got = weight_x(x) * wide(packed[n_y + j, x])
        for k in range(1, NX):
            got = got + weight_x(x_peer(k)) * wide(first_x[x_peer(k), j])
        sum_x[j] = got.astype(BF16)

    for k in range(1, NY):
        to = y_peer(k)
        piece = pl.ds(pl.multiple_of(to * PIECE, PIECE), PIECE)
        send(X2, sum_x.at[:, piece], second_x.at[y], device(x, to, z, c))

    if n_y:
        whole(Y1, first_y.at[pl.ds(0, NY - 1)]).wait_recv()

        @pl.loop(0, n_y, unroll=n_y)
        def _(j):
            got = weight_x(x) * wide(packed[j, y])
            for k in range(1, NY):
                got = got + weight_y(y_peer(k)) * wide(first_y[y_peer(k), j])
            sum_y[j] = got.astype(BF16)

        for k in range(1, NX):
            to = x_peer(k)
            piece = pl.ds(pl.multiple_of(to * PIECE, PIECE), PIECE)
            send(Y2, sum_y.at[:, piece], second_y.at[x], device(to, y, z, c))

    whole(E1, ebuf.at[pl.ds(0, NX - 1)]).wait_recv()
    diag = jnp.zeros((16, T), F32)
    for k in range(NX):
        diag = diag + wbuf[k:k + 1, :] * ebuf[k]
    eybuf[y] = diag

    @pl.loop(1, NY)
    def _(k):
        send(E2, eybuf.at[y], eybuf.at[y], device(x, y_peer(k), z, c))

    lane = lax.broadcasted_iota(jnp.int32, (PIECE, T), 1)
    row = lax.broadcasted_iota(jnp.int32, (PIECE, T), 0)

    def ridge(position):
        packed_row = position * PIECE + row
        on_diagonal = jnp.logical_and(packed_row >= 6 * T, packed_row % T == lane)
        return jnp.where(on_diagonal, RIDGE, 0.0).astype(F32)

    if n_y:
        whole(Y2, second_y.at[pl.ds(0, NX - 1)]).wait_recv()
        ridge_y = ridge(y * NX + x)

        @pl.loop(0, n_y, unroll=n_y)
        def _(j):
            got = wide(sum_y[j, pl.ds(pl.multiple_of(x * PIECE, PIECE), PIECE), :])
            for k in range(1, NX):
                got = got + wide(second_y[x_peer(k), j])
            stat[j] = (got + ridge_y).astype(BF16)

    whole(X2, second_x.at[pl.ds(0, NY - 1)]).wait_recv()
    ridge_x = ridge(x * NY + y)

    @pl.loop(0, n_x, unroll=n_x)
    def _(j):
        got = wide(sum_x[j, pl.ds(pl.multiple_of(y * PIECE, PIECE), PIECE), :])
        for k in range(1, NY):
            got = got + wide(second_x[y_peer(k), j])
        stat[n_y + j] = (got + ridge_x).astype(BF16)

    @pl.loop(0, CAP)
    def _(s):
        @pl.loop(1, NX * NY, unroll=5)
        def _(k):
            o = lax.rem(me + k, NX * NY)
            a2a_send[s, o] = stat[slot_idx[o * CAP + s]]
            send(A2A + s, a2a_send.at[s, o], pieces.at[s, me], {"dp": o, "blocks": col})

        pieces[s, me] = stat[slot_idx[me * CAP + s]]

    whole(E2, eybuf.at[pl.ds(0, NY - 1)]).wait_recv()
    diagonal = eybuf[0] + eybuf[1] + eybuf[2] + eybuf[3] + RIDGE
    diagonal_row = lax.broadcasted_iota(jnp.int32, (16, T), 0)
    unit5 = jnp.where(
        lax.broadcasted_iota(jnp.int32, (order, order), 0) == lax.broadcasted_iota(jnp.int32, (order, order), 1), 5.0, 0.0
    ).astype(F32)

    @pl.loop(0, CAP)
    def _(s):
        block = slot_idx[me * CAP + s]
        x_first = block >= n_y
        whole(A2A + s, a2a_send.at[0, pl.ds(0, NX * NY - 1)]).wait_recv()

        def tile(t):
            halves = []
            for p in (2 * t, 2 * t + 1):
                halves.append(jnp.where(x_first, wide(pieces[s, p]), wide(pieces[s, p % NX * NY + p // NX])))
            return jnp.concatenate(halves, axis=0)

        def put(r, k, value):
            mat[r * T:(r + 1) * T, k * T:(k + 1) * T] = value

        for t, (r, k) in enumerate(((2, 0), (2, 1), (3, 0), (3, 1), (1, 0), (3, 2))):
            value = tile(t)
            put(r, k, value)
            put(k, r, value.T)
        for h in range(2):
            value = tile(6 + h)
            turned = value.T
            edge = jnp.sum(jnp.where(diagonal_row == 2 * block + h, diagonal, 0.0), axis=0, keepdims=True)
            edge = wide(edge.astype(BF16))
            put(2 * h, 2 * h, jnp.where(lower, value, turned))
            put(2 * h + 1, 2 * h + 1, jnp.where(rows < cols, value, jnp.where(eye, edge, turned)))
        full = mat[...]
        z0 = 0.5 * order**0.5 * lax.rsqrt(jnp.sum(full * full, axis=(0, 1), keepdims=True) + 1e-06)
        coupled = z0 * full
        factor = ((unit5 - coupled) * 0.25).astype(BF16)
        iterate = (jnp.sqrt(jnp.sqrt(z0)) * wide(factor)).astype(BF16)
        square = product(factor, factor).astype(BF16)
        fourth = product(square, square).astype(BF16)
        coupled = product(fourth, coupled.astype(BF16))
        factor = ((unit5 - coupled) * 0.25).astype(BF16)
        root = product(iterate, factor)
        roots[s] = jnp.where(block < count, root, 0.0).astype(BF16)
        pltpu.make_async_copy(roots.at[s], out_ref.at[s], sems.at[0, OWN]).start()

    if nz > 1:
        whole(Z, zbuf.at[pl.ds(0, nz - 1)]).wait_send()
    whole(C, c_like).wait_send()
    whole(X1, first_x.at[pl.ds(0, NX - 1)]).wait_send()
    whole(X2, second_x.at[pl.ds(0, NY - 1)]).wait_send()
    if n_y:
        whole(Y1, first_y.at[pl.ds(0, NY - 1)]).wait_send()
        whole(Y2, second_y.at[pl.ds(0, NX - 1)]).wait_send()
    whole(E1, ebuf.at[pl.ds(0, NX - 1)]).wait_send()
    whole(E2, eybuf.at[pl.ds(0, NY - 1)]).wait_send()
    for s in range(CAP):
        whole(A2A + s, a2a_send.at[0, pl.ds(0, NX * NY - 1)]).wait_send()
    pltpu.make_async_copy(roots, out_ref, sems.at[0, OWN]).wait()


def body(n_blocks, grads, owner):
    count, order = grads.shape[1], grads.shape[2]
    entries = n_blocks * count * order * order
    n = NX * NY
    n_y = min(Y_FIRST, count - 1)
    n_x = count - n_y
    nz = n_blocks // NC
    dma = pltpu.SemaphoreType.DMA
    vmem = pltpu.VMEM
    roots = pl.pallas_call(
        functools.partial(exchange_kernel, n_blocks, count, float(entries)),
        out_shape=jax.ShapeDtypeStruct((CAP, order, order), BF16),
        in_specs=[pl.BlockSpec(memory_space=pl.ANY), pl.BlockSpec(memory_space=pl.ANY)],
        out_specs=pl.BlockSpec(memory_space=pl.ANY),
        scratch_shapes=[
            vmem((count, order, order), BF16),
            vmem((count, NX, QUARTER, T), BF16),
            vmem((NX, n_x, QUARTER, T), BF16),
            vmem((NY, max(n_y, 1), QUARTER, T), BF16),
            vmem((n_x, QUARTER, T), BF16),
            vmem((max(n_y, 1), QUARTER, T), BF16),
            vmem((NY, n_x, PIECE, T), BF16),
            vmem((NX, max(n_y, 1), PIECE, T), BF16),
            vmem((count + 1, PIECE, T), BF16),
            vmem((CAP, n, PIECE, T), BF16),
            vmem((CAP, n, PIECE, T), BF16),
            vmem((order, order), F32),
            vmem((CAP, order, order), BF16),
            vmem((nz, 8, T), F32),
            vmem(((NX + NY) * NC, 8, T), F32),
            vmem((NX + NY, T), F32),
            vmem((NX, 16, T), F32),
            vmem((NY, 16, T), F32),
            pltpu.SMEM((count,), jnp.int32),
            pltpu.SMEM((n * CAP,), jnp.int32),
            dma((count,)),
            dma((2, 9 + CAP)),
        ],
        compiler_params=pltpu.CompilerParams(
            collective_id=0, has_side_effects=True, vmem_limit_bytes=61 * 1024 * 1024
        ),
        cost_estimate=pl.CostEstimate(
            flops=2 * count * order**3 + 16 * order**3, bytes_accessed=grads.size * 2, transcendentals=0
        ),
        name="exchange",
    )(owner[:, 0], grads)
    return roots[None, None]


def solution(mesh):
    return jax.shard_map(
        functools.partial(body, mesh.shape["blocks"]),
        mesh=mesh,
        in_specs=(P("dp", "blocks", None, None), P("blocks", None)),
        out_specs=P("blocks", "dp", None, None, None),
        check_vma=False,
    )
```
